512 devices in a mesh: node: 16 (over z), tp: 32 (over x, y, core).
Axes of the slice: x: 4, y: 4, z: 16, core: 2. Of those that a mesh axis runs over, the one named last changes fastest.
Arguments:
- suffix_hidden: bfloat16 [4096, 7168], P('node', 'tp'), may hold values from -6 to 6
- suffix_adapter: int32 [16], replicated, may hold values from 0 to 3
- page_owner: int32 [16, 16, 1], replicated, may hold values from 0 to 15; in each aligned block of 16 rows (0 to 15, 16 to 31, ..., all dimensions but the last counted through in order) at most 2 rows name the same one
- page_number: int32 [16, 16], replicated, may hold values from 0 to 63
- prefix_page_count: int32 [16], replicated, may hold values from 8 to 16, as said below
- suffix_node: int32 [16], replicated, may hold values from 0 to 15, each once
- prefix_cache: bfloat16 [1024, 64, 576], P('node', 'tp'), may hold values from -210 to 210
- query_down_weight: bfloat16 [7168, 1536], P('tp'), may hold values from -0.0625 to 0.0625
- kv_down_weight: bfloat16 [7168, 576], P('tp'), may hold values from -0.0625 to 0.0625
- adapter_down_panels: bfloat16 [4, 7168, 64], P(None, 'tp'), may hold values from -0.0625 to 0.0625
- adapter_query_up: bfloat16 [4, 32, 1536], replicated, may hold values from -1 to 1
- adapter_kv_up: bfloat16 [4, 32, 576], replicated, may hold values from -1 to 1
- latent_query_gain: float32 [1536], replicated, may hold values from 0.25 to 2
- latent_kv_gain: float32 [512], replicated, may hold values from 0.25 to 2
- query_up_weight: bfloat16 [1536, 12288], P(None, 'tp'), may hold values from -0.15625 to 0.15625
- key_up_weight: bfloat16 [64, 128, 512], P('tp'), may hold values from -0.25 to 0.25
- value_up_weight: bfloat16 [64, 512, 128], P('tp'), may hold values from -0.25 to 0.25
Outputs:
- values: bfloat16 [4096, 8192], P('node', 'tp')
The draws below stay inside these ranges and needn't reach their ends.
Inputs may be any that keep to these rules, and one draw needn't show every extreme that they name: `page_owner`: among the 16 entries of one suffix's list no node is named more than 2 times, a bound that some block reaches. `prefix_page_count`: some suffix has exactly 16 pages. `suffix_node`: each node serves exactly one suffix.
All inputs are finite; a program needn't handle non-finite values.
Results may differ from the reference program's by a relative error of at most 0.035.
Values may be sent and summed in bfloat16 or wider, within the bound.
No kernel may reach another device: no remote copies, remote signals or barrier semaphores. Data moves between devices by JAX's collectives and lax.ppermute only.
A program may use at most 64 MiB of HBM per device.

```python
import math
import jax
import jax.numpy as jnp
import numpy as np
from jax import lax

MODEL_WIDTH = 7168
LATENT_Q_WIDTH = 1536
LATENT_KV_WIDTH = 512
ROTARY_WIDTH = 64
NOPE = 128
VDIM = 128
HEADS = 64
ADAPTER_RANK = 32
ADAPTER_COUNT = 4
PAGE = 64
MAXP = 16
SUFLEN = 256
POOL = 64
CAP = 2
SUFFIXES = 16
POOL_ALL = 1024
N_NODE = 16


def draw_prefix_page_count(key, part):
    key = jax.random.fold_in(key, 11)
    first, second = jax.random.split(key)
    lengths = jax.random.randint(first, (SUFFIXES,), MAXP // 2, MAXP + 1, dtype=jnp.int32)
    spot = jax.random.randint(second, (), 0, SUFFIXES, dtype=jnp.int32)
    return jnp.where(jnp.arange(SUFFIXES, dtype=jnp.int32) == spot, MAXP, lengths).astype(jnp.int32)


def draw_prefix_cache(key, part):
    key = jax.random.fold_in(key, 23)
    first = jax.random.fold_in(key, 0)
    array_shape = (POOL_ALL, PAGE, LATENT_KV_WIDTH + ROTARY_WIDTH)
    values = jnp.clip(jax.random.normal(first, array_shape, jnp.float32), -4.0, 4.0)
    return values.astype(jnp.bfloat16)


def set_ends(entries, stream_key, smallest, high):
    place = [jax.random.randint(jax.random.fold_in(stream_key, axis), (), 0, length) for axis, length in enumerate(entries.shape)]
    main_axis = entries.shape.index(max(entries.shape))
    beside = place[:main_axis] + [(place[main_axis] + 1) % entries.shape[main_axis]] + place[main_axis + 1:]
    return entries.at[tuple(place)].set(smallest).at[tuple(beside)].set(high)


def level_of(stream_key, shape, shards, least, high):
    level = 1.0
    for dim, parts in shards:
        draws = jax.random.uniform(jax.random.fold_in(jax.random.fold_in(stream_key, 6), dim), (parts,), jnp.float32, least / len(shards), high / len(shards))
        level = level * jnp.repeat(jnp.exp(draws), shape[dim] // parts).reshape((-1,) + (1,) * (len(shape) - 1 - dim))
    return level


def assign_block(rng, own, number, rows, count, top, limit, lean):
    order = jax.random.permutation(rng, count)
    crowded, common = shares(count, rows * top, limit, lean, True), shares(count, rows * top, limit, lean, False)
    places = jnp.arange(count)

    def named(tallies, turn):
        used = int((tallies > 0).sum())
        fixed = max(1, used // 4)
        passed = fixed + (places - fixed + turn * (used - fixed)) % max(1, count - fixed)
        return jnp.zeros((count,), jnp.int32).at[order[jnp.where(places < fixed, places, passed)]].set(jnp.asarray(tallies, jnp.int32))

    tallies = jnp.where(number % 4 == 0, named(crowded, number // 4), named(common, number - number // 4 - 1))
    mixed = jax.random.permutation(jax.random.fold_in(own, 3), count)
    source_of, sink = mixed[0:count // 2 * 2:2], mixed[1:count // 2 * 2:2]
    slack = jnp.minimum(tallies[source_of] - 1, limit - tallies[sink]) // 2
    slack = jnp.where((source_of == order[0]) | (sink == order[0]) | (tallies[sink] == 0), 0, jnp.maximum(slack, 0))
    passed = jax.random.randint(jax.random.fold_in(own, 4), (count // 2,), 0, 1 << 20) % (slack + 1)
    tallies = tallies.at[source_of].add(-passed).at[sink].add(passed)
    labels = jnp.searchsorted(jnp.cumsum(tallies), jnp.arange(rows * top), side="right").astype(jnp.int32)
    table = labels.reshape(top, rows).T
    table = table[jax.random.permutation(jax.random.fold_in(own, 1), rows)]
    turn = jax.random.randint(jax.random.fold_in(own, 2), (rows, 1), 0, top)
    return jnp.take_along_axis(table, (jnp.arange(top)[None, :] + turn) % top, axis=1)


def shares(number_of, total, most, lean, full):
    portions = [(1 << 20) // math.isqrt(rank ** lean) + 1 for rank in range(1, number_of + 1)]
    largest = most if full else min(most, max(-(-total // number_of), total * portions[0] // sum(portions)))
    least = 1 if total - largest >= number_of - 1 else 0
    given, spare = [largest] + [least] * (number_of - 1), total - largest - least * (number_of - 1)
    while spare > 0:
        free = [i for i in range(1, number_of) if given[i] < largest] or [i for i in range(1, number_of) if given[i] < most]
        pool, budget = sum([portions[i] for i in free]), spare
        for i in free:
            more = min(most - given[i], max(1, budget * portions[i] // pool), spare)
            given[i] = given[i] + more
            spare = spare - more
    return np.array(given)


def bell_draw(own_key, extent, spread, limit, pieces=(), kind=jnp.bfloat16):
    result = jax.random.normal(own_key, extent, jnp.float32) * spread
    if len(pieces) > 0:
        result = level_of(own_key, extent, pieces, -0.22, 0.18) * result
    return jnp.clip(result, min=-limit, max=limit).astype(kind)


def setup_inputs(seed: int = 0) -> dict:
    key_of = jax.random.split(jax.random.key(seed), 18)
    suffix_hidden = bell_draw(key_of[0], (N_NODE * SUFLEN, MODEL_WIDTH), 1.0, 6.0, ((0, 16), (1, 32)))
    suffix_adapter = set_ends(jax.random.randint(key_of[1], (SUFFIXES,), 0, ADAPTER_COUNT), jax.random.fold_in(key_of[1], 1), 0, ADAPTER_COUNT - 1).astype(jnp.int32)
    page_owner_keys = jax.random.split(jax.random.fold_in(key_of[2], 1), SUFFIXES * MAXP // MAXP)
    page_owner_turns = jax.random.permutation(jax.random.fold_in(key_of[2], 3), SUFFIXES * MAXP // MAXP)
    page_owner = jax.vmap(lambda own, number: assign_block(jax.random.fold_in(key_of[2], 2), own, number, MAXP, N_NODE, 1, CAP, 1))(page_owner_keys, page_owner_turns).reshape((SUFFIXES, MAXP, 1))
    page_number = set_ends(jax.random.randint(key_of[3], (SUFFIXES, MAXP), 0, POOL), jax.random.fold_in(key_of[3], 1), 0, POOL - 1).astype(jnp.int32)
    prefix_page_count = draw_prefix_page_count(jax.random.fold_in(key_of[17], 71), 0)
    suffix_node = jax.random.permutation(key_of[5], N_NODE).astype(jnp.int32)
    prefix_cache = draw_prefix_cache(jax.random.fold_in(key_of[17], 71), 0)
    query_down_weight = bell_draw(key_of[7], (MODEL_WIDTH, LATENT_Q_WIDTH), MODEL_WIDTH ** -0.5, 0.0625, ((0, 32),))
    kv_down_weight = bell_draw(key_of[8], (MODEL_WIDTH, LATENT_KV_WIDTH + ROTARY_WIDTH), MODEL_WIDTH ** -0.5, 0.0625, ((0, 32),))
    adapter_down_panels = bell_draw(key_of[9], (ADAPTER_COUNT, MODEL_WIDTH, 2 * ADAPTER_RANK), MODEL_WIDTH ** -0.5, 0.0625, ((1, 32),))
    adapter_query_up = bell_draw(key_of[10], (ADAPTER_COUNT, ADAPTER_RANK, LATENT_Q_WIDTH), ADAPTER_RANK ** -0.5, 1.0)
    adapter_kv_up = bell_draw(key_of[11], (ADAPTER_COUNT, ADAPTER_RANK, LATENT_KV_WIDTH + ROTARY_WIDTH), ADAPTER_RANK ** -0.5, 1.0)
    latent_query_gain = jnp.clip(jax.random.uniform(key_of[12], (LATENT_Q_WIDTH,), jnp.float32, 0.25, 2.0), 0.25, 2.0)
    latent_kv_gain = jnp.clip(jax.random.uniform(key_of[13], (LATENT_KV_WIDTH,), jnp.float32, 0.25, 2.0), 0.25, 2.0)
    query_up_weight = bell_draw(key_of[14], (LATENT_Q_WIDTH, HEADS * (NOPE + ROTARY_WIDTH)), LATENT_Q_WIDTH ** -0.5, 0.15625, ((1, 32),))
    key_up_weight = bell_draw(key_of[15], (HEADS, NOPE, LATENT_KV_WIDTH), LATENT_KV_WIDTH ** -0.5, 0.25, ((0, 32),))
    value_up_weight = bell_draw(key_of[16], (HEADS, LATENT_KV_WIDTH, VDIM), LATENT_KV_WIDTH ** -0.5, 0.25, ((0, 32),))
    return {"suffix_hidden": suffix_hidden, "suffix_adapter": suffix_adapter, "page_owner": page_owner, "page_number": page_number, "prefix_page_count": prefix_page_count, "suffix_node": suffix_node, "prefix_cache": prefix_cache, "query_down_weight": query_down_weight, "kv_down_weight": kv_down_weight, "adapter_down_panels": adapter_down_panels, "adapter_query_up": adapter_query_up, "adapter_kv_up": adapter_kv_up, "latent_query_gain": latent_query_gain, "latent_kv_gain": latent_kv_gain, "query_up_weight": query_up_weight, "key_up_weight": key_up_weight, "value_up_weight": value_up_weight}


def rope_apply(vectors, token_positions):
    half = vectors.shape[1] // 2
    steps = jnp.arange(half, dtype=jnp.float32)
    freqs = jnp.power(jnp.float32(10000.0), -2.0 * steps / vectors.shape[1])
    angles = token_positions[:, None] * freqs[None, :]
    first = vectors[:, :half]
    second = vectors[:, half:]
    cosine = jnp.cos(angles)
    sine = jnp.sin(angles)
    return jnp.concatenate([first * cosine - second * sine, first * sine + second * cosine], axis=1)

def normalize(vectors, gain):
    mean_square = lax.optimization_barrier(jnp.mean(vectors * vectors, axis=1, keepdims=True))
    return vectors * lax.rsqrt(mean_square + 1e-06) * gain[None, :]

def finalize(unnormed, adapter_choice, token_positions, adapter_query_up, adapter_kv_up, latent_query_gain, latent_kv_gain):
    latent_query_span = adapter_query_up.shape[2]
    latent_kv_span = adapter_kv_up.shape[2]
    adapter_rank = adapter_query_up.shape[1]
    latent = latent_kv_gain.shape[0]
    lowrank = unnormed[:, latent_query_span + latent_kv_span:].astype(jnp.bfloat16)
    query_panel = lax.dynamic_index_in_dim(adapter_query_up, adapter_choice, 0, keepdims=False)
    kv_panel = lax.dynamic_index_in_dim(adapter_kv_up, adapter_choice, 0, keepdims=False)
    q_raw = unnormed[:, :latent_query_span] + jnp.dot(lowrank[:, :adapter_rank], query_panel, preferred_element_type=jnp.float32)
    kv_raw = unnormed[:, latent_query_span:latent_query_span + latent_kv_span] + jnp.dot(lowrank[:, adapter_rank:], kv_panel, preferred_element_type=jnp.float32)
    query_latent = normalize(q_raw, latent_query_gain).astype(jnp.bfloat16)
    compressed = normalize(kv_raw[:, :latent], latent_kv_gain)
    rotated = rope_apply(kv_raw[:, latent:], token_positions)
    local_keys = jnp.concatenate([compressed, rotated], axis=1).astype(jnp.bfloat16)
    return (query_latent, local_keys)

def attend(query, prefix_keys, prefix_valid, local_keys, scale, latent):
    contract = (((1,), (1,)), ((), ()))
    far = lax.dot_general(query, prefix_keys, contract, preferred_element_type=jnp.float32) * scale
    near = lax.dot_general(query, local_keys, contract, preferred_element_type=jnp.float32) * scale
    far = jnp.where(prefix_valid[None, :], far, -jnp.inf)
    count = query.shape[0]
    places = jnp.arange(count, dtype=jnp.int32)
    near = jnp.where(places[:, None] >= places[None, :], near, -jnp.inf)
    top = jnp.maximum(lax.optimization_barrier(jnp.max(far, axis=1)), lax.optimization_barrier(jnp.max(near, axis=1)))
    far_exp = jnp.exp(far - top[:, None])
    near_exp = jnp.exp(near - top[:, None])
    total = lax.optimization_barrier(jnp.sum(far_exp, axis=1)) + lax.optimization_barrier(jnp.sum(near_exp, axis=1))
    mixed = jnp.dot(far_exp.astype(jnp.bfloat16), prefix_keys[:, :latent], preferred_element_type=jnp.float32)
    mixed = mixed + jnp.dot(near_exp.astype(jnp.bfloat16), local_keys[:, :latent], preferred_element_type=jnp.float32)
    return (mixed / total[:, None]).astype(jnp.bfloat16)

def head_output(q_head, token_positions, key_up, value_up, prefix_keys, prefix_valid, local_keys, scale):
    nope = key_up.shape[0]
    q_rope = rope_apply(q_head[:, nope:].astype(jnp.float32), token_positions).astype(jnp.bfloat16)
    q_abs = jnp.dot(q_head[:, :nope], key_up, preferred_element_type=jnp.float32).astype(jnp.bfloat16)
    query = jnp.concatenate([q_abs, q_rope], axis=1)
    latent_out = attend(query, prefix_keys, prefix_valid, local_keys, scale, key_up.shape[1])
    return jnp.dot(latent_out, value_up, preferred_element_type=jnp.float32).astype(jnp.bfloat16)

def reference(suffix_hidden, suffix_adapter, page_owner, page_number, prefix_page_count, suffix_node, prefix_cache, query_down_weight, kv_down_weight, adapter_down_panels, adapter_query_up, adapter_kv_up, latent_query_gain, latent_kv_gain, query_up_weight, key_up_weight, value_up_weight):
    order = jnp.arange(N_NODE, dtype=jnp.int32)
    suffix_at = lax.optimization_barrier(jnp.sum(jnp.where(suffix_node[None, :] == order[:, None], order[None, :], 0), axis=1)).astype(jnp.int32)
    scale = 1.0 / math.sqrt(NOPE + ROTARY_WIDTH)
    head_width = NOPE + ROTARY_WIDTH

    def one_node(node):
        mine = suffix_at[node]
        adapter_choice = suffix_adapter[mine]
        length = prefix_page_count[mine]
        token_rows = lax.dynamic_slice_in_dim(suffix_hidden, (node * SUFLEN).astype(jnp.int32), SUFLEN, 0)
        adapter_local = lax.dynamic_index_in_dim(adapter_down_panels, adapter_choice, 0, keepdims=False)
        unnormed = jnp.concatenate([jnp.dot(token_rows, query_down_weight, preferred_element_type=jnp.float32), jnp.dot(token_rows, kv_down_weight, preferred_element_type=jnp.float32), jnp.dot(token_rows, adapter_local, preferred_element_type=jnp.float32)], axis=1)
        token_positions = (length * PAGE + jnp.arange(SUFLEN, dtype=jnp.int32)).astype(jnp.float32)
        query_latent, local_keys = finalize(unnormed, adapter_choice, token_positions, adapter_query_up, adapter_kv_up, latent_query_gain, latent_kv_gain)
        page_ids = (page_owner[mine, :, 0] * POOL + page_number[mine]).astype(jnp.int32)
        prefix_keys = jnp.take(prefix_cache, page_ids, axis=0).reshape(MAXP * PAGE, LATENT_KV_WIDTH + ROTARY_WIDTH)
        prefix_valid = jnp.repeat(jnp.arange(MAXP, dtype=jnp.int32) < length, PAGE)
        q_all = jnp.dot(query_latent, query_up_weight, preferred_element_type=jnp.float32).astype(jnp.bfloat16)

        def one_head(head):
            q_head = lax.dynamic_slice_in_dim(q_all, (head * head_width).astype(jnp.int32), head_width, 1)
            return head_output(q_head, token_positions, key_up_weight[head], value_up_weight[head], prefix_keys, prefix_valid, local_keys, scale)
        per_head = lax.map(one_head, jnp.arange(HEADS, dtype=jnp.int32))
        return jnp.transpose(per_head, (1, 0, 2)).reshape(SUFLEN, HEADS * VDIM)
    outputs = lax.map(one_node, order)
    return outputs.reshape(N_NODE * SUFLEN, HEADS * VDIM)
```

```python
import math

import jax
import jax.numpy as jnp
import numpy as np
from jax import lax
from jax.experimental import pallas as pl
from jax.experimental.pallas import tpu as pltpu
from jax.sharding import Mesh
from jax.sharding import PartitionSpec as P

F32 = jnp.float32
BF16 = jnp.bfloat16

PAGE = 64
MAXP = 16
SUFLEN = 256
NODES = 16
CHIPS = 16
HALF = SUFLEN // 2
ROWS = HALF // CHIPS
Q = 1536
LATENT = 512
ROPE = 64
KEY = LATENT + ROPE
RANK = 32
DOWN = Q + KEY + 2 * RANK
CHUNKS = 4
PAGEW = 640
GROUPS = 1 + CHUNKS
ROPES = Q + GROUPS * LATENT
BLOCK = ROPES + 3 * 128
SENDS = ((0, 1024), (1024, DOWN))
NOPE = 128
HEADW = NOPE + ROPE
VDIM = 128

FACTOR = math.log2(math.e) / math.sqrt(HEADW)
NT = (((1,), (1,)), ((), ()))
VMEM = pl.BlockSpec(memory_space=pltpu.VMEM)
HBM = pl.BlockSpec(memory_space=pltpu.HBM)
SMEM = pl.BlockSpec(memory_space=pltpu.SMEM)


def mm(a, b):
    return jnp.dot(a, b, preferred_element_type=F32)


def mmt(a, b):
    return lax.dot_general(a, b, NT, preferred_element_type=F32)


def iota(shape, dim):
    return lax.broadcasted_iota(jnp.int32, shape, dim)


def rope_tables():
    freqs = 10000.0 ** (-2.0 * np.arange(ROPE // 2) / ROPE)
    lanes = np.tile(freqs, 4)[None, :]
    base = np.arange(MAXP + 1)[:, None] * PAGE * lanes
    step = np.arange(SUFLEN)[:, None] * lanes
    return [t.astype(np.float32) for t in (np.cos(base), np.sin(base), np.cos(step), np.sin(step))]


def my_suffix(node_ref):
    me = lax.axis_index("node")
    mine = jnp.int32(0)
    for s in range(NODES):
        mine = jnp.where(node_ref[s] == me, s, mine)
    return me, mine


def down_kernel(
    node_hbm, adapter_hbm, x_hbm, wq_hbm, wkv_hbm, panels_hbm, keep_ref, *refs
):
    send_refs, (node_ref, adapter_ref, x_ref, wq_ref, wkv_ref, panels_ref, sems) = refs[: len(SENDS)], refs[len(SENDS) :]
    sources = (x_hbm, wq_hbm, wkv_hbm, panels_hbm, node_hbm, adapter_hbm)
    targets = (x_ref, wq_ref, wkv_ref, panels_ref, node_ref, adapter_ref)
    copies = [pltpu.make_async_copy(src, dst, sems.at[i]) for i, (src, dst) in enumerate(zip(sources, targets))]
    for copy in copies:
        copy.start()
    for copy in copies:
        copy.wait()
    _, mine = my_suffix(node_ref)
    core = lax.axis_index("core")
    x = x_ref[...].T
    cut = SENDS[0][1]
    tail = [mm(x, wq_ref[:, cut:]), mm(x, wkv_ref[...]), mmt(x, panels_ref[adapter_ref[mine]])]
    parts = [mm(x, wq_ref[:, :cut]), jnp.concatenate(tail, axis=1)]

    @pl.when(core == 0)
    def _():
        for (lo, hi), part, send_ref in zip(SENDS, parts, send_refs):
            keep_ref[:, lo:hi] = part[:HALF]
            send_ref[...] = part[HALF:]

    @pl.when(core != 0)
    def _():
        for (lo, hi), part, send_ref in zip(SENDS, parts, send_refs):
            keep_ref[:, lo:hi] = part[HALF:]
            send_ref[...] = part[:HALF]


def pages_kernel(node_hbm, owner_hbm, number_hbm, cache_hbm, pages_ref, node_row, owner_ref, number_ref, cache_ref, sems):
    copies = [
        pltpu.make_async_copy(source, target, sems.at[i])
        for i, (source, target) in enumerate(
            [(cache_hbm, cache_ref), (node_hbm, node_row), (owner_hbm, owner_ref), (number_hbm, number_ref)]
        )
    ]
    for copy in copies:
        copy.start()
    for copy in copies[1:]:
        copy.wait()
    me = lax.axis_index("node")
    count = NODES * 8
    node_of = iota((count, NODES), 0) // 8
    within = iota((count, 1), 0) % 8
    slot = within // 2
    expand = (node_row[...] == node_of).astype(BF16)
    owner = mm(expand, owner_ref[...].reshape(NODES, MAXP).astype(BF16))
    number = mm(expand, number_ref[...].astype(BF16))
    held = owner == me.astype(F32)
    before = (iota((MAXP, MAXP), 0) < iota((MAXP, MAXP), 1)).astype(BF16)
    rank = mm(held.astype(BF16), before)
    picked = held & (rank == slot.astype(F32))
    page = jnp.sum(jnp.where(picked, number + 1.0, 0.0), axis=1, keepdims=True).astype(jnp.int32) - 1
    row = 2 * page + within % 2
    select = (iota((count, 128), 1) == row) & (page >= 0)
    copies[0].wait()
    pages_ref[:, :KEY] = mm(select.astype(BF16), cache_ref[...].reshape(128, KEY)).astype(BF16)
    pages_ref[:, KEY:] = jnp.zeros((count, PAGEW - KEY), BF16)


def add_kernel(keep_ref, *refs):
    *swapped_refs, out_ref = refs
    for (lo, hi), swapped_ref in zip(SENDS, swapped_refs):
        out_ref[:, lo:hi] = (keep_ref[:, lo:hi] + swapped_ref[...]).astype(BF16)


def angles(length, rows, cb_ref, sb_ref, ct_ref, st_ref):
    cb = cb_ref[pl.ds(length, 1), :]
    sb = sb_ref[pl.ds(length, 1), :]
    ct = ct_ref[rows, :]
    st = st_ref[rows, :]
    return cb * ct - sb * st, sb * ct + cb * st


def turn(v):
    half = ROPE // 2
    parts = []
    for g in range(v.shape[1] // ROPE):
        parts.append(-v[:, g * ROPE + half : (g + 1) * ROPE])
        parts.append(v[:, g * ROPE : g * ROPE + half])
    return jnp.concatenate(parts, axis=1)


def finish_kernel(
    node_ref,
    adapter_ref,
    length_ref,
    node_row,
    owner_ref,
    parts_ref,
    pages_ref,
    aq_ref,
    akv_ref,
    gq_ref,
    gkv_ref,
    cb_ref,
    sb_ref,
    ct_ref,
    st_ref,
    out_ref,
):
    me, mine = my_suffix(node_ref)
    adapter = adapter_ref[mine]
    length = length_ref[mine]
    core = lax.axis_index("core")
    chip = lax.axis_index("x") * 4 + lax.axis_index("y")
    first = pl.multiple_of(core * HALF + chip * ROWS, ROWS)
    down = parts_ref[0].astype(F32)
    for i in range(1, CHIPS):
        down = down + parts_ref[i].astype(F32)
    low = down[:, Q + KEY :].astype(BF16)
    q_raw = down[:, :Q] + mm(low[:, :RANK], aq_ref[adapter])
    kv_raw = down[:, Q : Q + KEY] + mm(low[:, RANK:], akv_ref[adapter])
    q_lat = q_raw * lax.rsqrt(jnp.mean(q_raw * q_raw, axis=1, keepdims=True) + 1e-06) * gq_ref[...][None, :]
    c = kv_raw[:, :LATENT]
    c = c * lax.rsqrt(jnp.mean(c * c, axis=1, keepdims=True) + 1e-06) * gkv_ref[...][None, :]
    k = kv_raw[:, LATENT:]
    cosine, sine = angles(length, pl.ds(first, ROWS), cb_ref, sb_ref, ct_ref, st_ref)
    k = k * cosine[:, :ROPE] + turn(k) * sine[:, :ROPE]

    count = MAXP * 2
    pick = (node_row[...] == me).astype(BF16)
    mine_owner = mm(pick, owner_ref[...].reshape(NODES, MAXP).astype(BF16))
    entry = iota((count, MAXP), 0) // 2
    lane = iota((count, MAXP), 1)
    holder = jnp.sum(jnp.where(lane == entry, mine_owner, 0.0), axis=1, keepdims=True)
    earlier = (mine_owner == holder) & (lane < entry)
    rank = jnp.sum(earlier.astype(F32), axis=1, keepdims=True)
    source = holder.astype(jnp.int32) * 8 + rank.astype(jnp.int32) * 2 + iota((count, 1), 0) % 2
    select = (iota((count, 128), 1) == source).astype(BF16)
    prefix = mm(select, pages_ref[...])[:, :KEY]
    chunks = [prefix[g * ROWS : (g + 1) * ROWS] for g in range(CHUNKS)]
    pieces = [q_lat, c] + [p[:, :LATENT] for p in chunks]
    pieces += [k] + [p[:, LATENT:] for p in chunks] + [jnp.zeros((ROWS, ROPE), F32)]
    block = jnp.concatenate(pieces, axis=1).astype(BF16)
    for i in range(CHIPS):
        out_ref[i] = block


def attend_kernel(
    node_ref, length_ref, mine_ref, other_ref, wq_ref, wk_ref, wv_ref, cb_ref, sb_ref, ct_ref, st_ref, out_ref
):
    _, mine = my_suffix(node_ref)
    length = length_ref[mine]
    core = lax.axis_index("core")
    rows_a = pl.ds(pl.multiple_of(core * HALF, HALF), HALF)
    rows_b = pl.ds(pl.multiple_of((1 - core) * HALF, HALF), HALF)

    def both(lo, hi):
        return jnp.concatenate([mine_ref[:, lo:hi], other_ref[:, lo:hi]], axis=0)

    q_all = mm(both(0, Q), wq_ref[...]).astype(BF16)
    ca, sa = angles(length, rows_a, cb_ref, sb_ref, ct_ref, st_ref)
    cb, sb = angles(length, rows_b, cb_ref, sb_ref, ct_ref, st_ref)
    cosine = jnp.concatenate([ca, cb], axis=0)
    sine = jnp.concatenate([sa, sb], axis=0)
    ropes = jnp.concatenate([q_all[:, NOPE:HEADW], q_all[:, HEADW + NOPE :]], axis=1).astype(F32)
    ropes = (ropes * cosine + turn(ropes) * sine).astype(BF16)
    rope = jnp.concatenate([ropes[:, :ROPE], ropes[:, ROPE:]], axis=0)
    zero = jnp.zeros_like(rope)
    absorbed = [mm(q_all[:, h * HEADW : h * HEADW + NOPE], wk_ref[h]).astype(BF16) for h in range(2)]
    absorbed = jnp.concatenate(absorbed, axis=0)
    query = (jnp.concatenate([absorbed, rope, zero], axis=1), jnp.concatenate([absorbed, zero, rope], axis=1))
    latents = [both(Q + g * LATENT, Q + (g + 1) * LATENT) for g in range(GROUPS)]

    count = 2 * SUFLEN
    place = iota((count, SUFLEN), 0) % SUFLEN
    place = jnp.where(place < HALF, place + core * HALF, place - core * HALF)
    spot = iota((count, SUFLEN), 1)
    page = (spot % 8) // 2
    spot = jnp.where(spot < HALF, spot + core * HALF, spot - core * HALF)
    scores = []
    for g in range(GROUPS):
        tile = ROPES + g // 2 * 128
        s = mmt(query[g % 2], jnp.concatenate([latents[g], both(tile, tile + 128)], axis=1))
        if g == 0:
            s = jnp.where(place >= spot, s, -jnp.inf)
        elif g > 2:
            s = jnp.where(page + 4 * (g - 1) < length, s, -jnp.inf)
        scores.append(s)
    top = scores[0]
    for s in scores[1:]:
        top = jnp.maximum(top, s)
    top = jnp.max(top, axis=1, keepdims=True)
    weights = [jnp.exp2((s - top) * FACTOR) for s in scores]
    total = weights[0]
    for w in weights[1:]:
        total = total + w
    total = jnp.sum(total, axis=1, keepdims=True)
    mixed = jnp.zeros((count, LATENT), F32)
    for g in range(GROUPS):
        mixed = mixed + mm(weights[g].astype(BF16), latents[g])
    latent = (mixed / total).astype(BF16)
    for h in range(2):
        values = mm(latent[h * SUFLEN : (h + 1) * SUFLEN], wv_ref[h]).astype(BF16)
        out_ref[rows_a, h * VDIM : (h + 1) * VDIM] = values[:HALF]
        out_ref[rows_b, h * VDIM : (h + 1) * VDIM] = values[HALF:]


def on_device(
    suffix_hidden,
    suffix_adapter,
    page_owner,
    page_number,
    prefix_page_count,
    suffix_node,
    prefix_cache,
    query_down_weight,
    kv_down_weight,
    adapter_down_panels,
    adapter_query_up,
    adapter_kv_up,
    latent_query_gain,
    latent_kv_gain,
    query_up_weight,
    key_up_weight,
    value_up_weight,
):
    alone = pltpu.CompilerParams(vmem_limit_bytes=60 * 1024 * 1024)
    params = pltpu.CompilerParams(vmem_limit_bytes=40 * 1024 * 1024)
    tables = [jnp.asarray(t) for t in rope_tables()]
    owner = jnp.transpose(page_owner, (0, 2, 1))
    node_row = suffix_node.reshape(1, NODES)
    swap = [(0, 1), (1, 0)]

    outgoing = pl.pallas_call(
        pages_kernel,
        out_shape=jax.ShapeDtypeStruct((NODES * 8, PAGEW), BF16),
        in_specs=[HBM] * 4,
        out_specs=VMEM,
        scratch_shapes=[
            pltpu.VMEM((1, NODES), jnp.int32),
            pltpu.VMEM((NODES, 1, MAXP), jnp.int32),
            pltpu.VMEM((NODES, MAXP), jnp.int32),
            pltpu.VMEM(prefix_cache.shape, BF16),
            pltpu.SemaphoreType.DMA((4,)),
        ],
        compiler_params=alone,
        cost_estimate=pl.CostEstimate(flops=20_000_000, bytes_accessed=300_000, transcendentals=0),
        name="pages",
    )(node_row, owner, page_number, prefix_cache)
    received = lax.all_to_all(outgoing.reshape(NODES, 8, PAGEW), "node", 0, 0, tiled=True)
    hidden, _ = lax.optimization_barrier((suffix_hidden, outgoing))
    keep, *send = pl.pallas_call(
        down_kernel,
        out_shape=[jax.ShapeDtypeStruct((HALF, DOWN), F32)] + [jax.ShapeDtypeStruct((HALF, hi - lo), F32) for lo, hi in SENDS],
        in_specs=[HBM] * 6,
        out_specs=[VMEM] * (1 + len(SENDS)),
        scratch_shapes=[
            pltpu.SMEM((NODES,), jnp.int32),
            pltpu.SMEM((NODES,), jnp.int32),
            pltpu.VMEM((224, SUFLEN), BF16),
            pltpu.VMEM((224, Q), BF16),
            pltpu.VMEM((224, KEY), BF16),
            pltpu.VMEM((4, 2 * RANK, 224), BF16),
            pltpu.SemaphoreType.DMA((6,)),
        ],
        compiler_params=alone,
        cost_estimate=pl.CostEstimate(flops=1000, bytes_accessed=1000, transcendentals=0),
        name="down",
    )(
        suffix_node,
        suffix_adapter,
        hidden.T,
        query_down_weight,
        kv_down_weight,
        jnp.transpose(adapter_down_panels, (0, 2, 1)),
    )
    swapped = [lax.ppermute(part, "core", swap) for part in send]
    partial = pl.pallas_call(
        add_kernel,
        out_shape=jax.ShapeDtypeStruct((HALF, DOWN), BF16),
        in_specs=[VMEM] * (1 + len(SENDS)),
        out_specs=VMEM,
        compiler_params=params,
        cost_estimate=pl.CostEstimate(flops=1000, bytes_accessed=1000, transcendentals=0),
        name="add",
    )(keep, *swapped).reshape(CHIPS, ROWS, DOWN)
    parts = lax.all_to_all(partial, ("x", "y"), 0, 0, tiled=True)

    block = pl.pallas_call(
        finish_kernel,
        out_shape=jax.ShapeDtypeStruct((CHIPS, ROWS, BLOCK), BF16),
        in_specs=[SMEM] * 3 + [VMEM] * 12,
        out_specs=VMEM,
        compiler_params=params,
        name="finish",
    )(
        suffix_node,
        suffix_adapter,
        prefix_page_count,
        node_row,
        owner,
        parts,
        received.reshape(NODES * 8, PAGEW),
        adapter_query_up,
        adapter_kv_up,
        latent_query_gain,
        latent_kv_gain,
        *tables,
    )
    gathered = lax.all_to_all(block, ("x", "y"), 0, 0, tiled=True).reshape(HALF, BLOCK)
    other = lax.ppermute(gathered, "core", swap)
    return pl.pallas_call(
        attend_kernel,
        out_shape=jax.ShapeDtypeStruct((SUFLEN, 2 * VDIM), BF16),
        in_specs=[SMEM] * 2 + [VMEM] * 9,
        out_specs=VMEM,
        compiler_params=params,
        name="attend",
    )(
        suffix_node,
        prefix_page_count,
        gathered,
        other,
        query_up_weight,
        key_up_weight,
        value_up_weight,
        *tables,
    )


def solution(mesh):
    inner = Mesh(mesh.devices.reshape(NODES, 4, 4, 2), ("node", "x", "y", "core"))
    tp = ("x", "y", "core")
    return jax.shard_map(
        on_device,
        mesh=inner,
        in_specs=(
            P("node", tp),
            P(),
            P(),
            P(),
            P(),
            P(),
            P("node", tp, None),
            P(tp, None),
            P(tp, None),
            P(None, tp, None),
            P(),
            P(),
            P(),
            P(),
            P(None, tp),
            P(tp, None, None),
            P(tp, None, None),
        ),
        out_specs=P("node", tp),
        check_vma=False,
    )
```

```python
import math

import jax
import jax.numpy as jnp
import numpy as np
from jax import lax
from jax.experimental import pallas as pl
from jax.experimental.pallas import tpu as pltpu
from jax.sharding import PartitionSpec as P

F32 = jnp.float32
BF16 = jnp.bfloat16

PAGE = 64
MAXP = 16
SUFLEN = 256
NODES = 16
CHIPS = 16
HALF = SUFLEN // 2
ROWS = HALF // CHIPS
Q = 1536
LATENT = 512
ROPE = 64
KEY = LATENT + ROPE
RANK = 32
DOWN = Q + KEY + 2 * RANK
CHUNKS = 4
PAGEW = 640
ROOT = 12
CORNER = (2, 2)
PLANE = [[((CORNER[0] + k // 4) % 4 * 4 + (CORNER[1] + k % 4) % 4) * 2 + c for k in range(CHIPS)] for c in range(2)]
RING = [(ROOT + i) % NODES for i in range(NODES)]
GROUPS = 1 + CHUNKS
ROPES = Q + GROUPS * LATENT
BLOCK = ROPES + 3 * 128
SENDS = ((0, 1024), (1024, DOWN))
NOPE = 128
HEADW = NOPE + ROPE
VDIM = 128

FACTOR = math.log2(math.e) / math.sqrt(HEADW)
NT = (((1,), (1,)), ((), ()))
VMEM = pl.BlockSpec(memory_space=pltpu.VMEM)
HBM = pl.BlockSpec(memory_space=pltpu.HBM)


def mm(a, b):
    return jnp.dot(a, b, preferred_element_type=F32)


def mmt(a, b):
    return lax.dot_general(a, b, NT, preferred_element_type=F32)


def iota(shape, dim):
    return lax.broadcasted_iota(jnp.int32, shape, dim)


def rope_tables():
    freqs = 10000.0 ** (-2.0 * np.arange(ROPE // 2) / ROPE)
    lanes = np.tile(freqs, 4)[None, :]
    base = np.arange(MAXP + 1)[:, None] * PAGE * lanes
    step = np.arange(SUFLEN)[:, None] * lanes
    return [t.astype(np.float32) for t in (np.cos(base), np.sin(base), np.cos(step), np.sin(step))]


def mine_of(row_ref, node_row):
    served = node_row[...] == lax.axis_index("node")
    return jnp.sum(jnp.where(served, row_ref[...], 0), axis=1, keepdims=True)


def load(sources, targets, sems):
    copies = [pltpu.make_async_copy(src, dst, sems.at[i]) for i, (src, dst) in enumerate(zip(sources, targets))]
    for copy in copies:
        copy.start()
    return copies


def down_kernel(node_hbm, adapter_hbm, x_hbm, wq_hbm, wkv_hbm, panels_hbm, keep_ref, *refs):
    send_refs, scratch, sems = refs[: len(SENDS)], refs[len(SENDS) : -1], refs[-1]
    node_row, adapter_row, x_ref, wq_ref, wkv_ref, panels_ref = scratch
    copies = load((x_hbm, wq_hbm, wkv_hbm, panels_hbm, node_hbm, adapter_hbm), (x_ref, wq_ref, wkv_ref, panels_ref, node_row, adapter_row), sems)
    core = lax.axis_index("tp") % 2
    copies[0].wait()
    x = x_ref[...].T
    copies[1].wait()
    parts = [mm(x, wq_ref[:, lo : min(hi, Q)]) if lo < Q else None for lo, hi in SENDS]
    for copy in copies[2:]:
        copy.wait()
    adapter = mine_of(adapter_row, node_row)
    panel = jnp.zeros(panels_ref.shape[1:], F32)
    for i in range(panels_ref.shape[0]):
        panel = jnp.where(adapter == i, panels_ref[i].astype(F32), panel)
    tail = [mm(x, wkv_ref[...]), mmt(x, panel.astype(BF16))]
    parts[-1] = jnp.concatenate([parts[-1]] * (SENDS[-1][0] < Q) + tail, axis=1)

    @pl.when(core == 0)
    def _():
        for (lo, hi), part, send_ref in zip(SENDS, parts, send_refs):
            keep_ref[:, lo:hi] = part[:HALF]
            send_ref[...] = part[HALF:]

    @pl.when(core != 0)
    def _():
        for (lo, hi), part, send_ref in zip(SENDS, parts, send_refs):
            keep_ref[:, lo:hi] = part[HALF:]
            send_ref[...] = part[:HALF]


def pages_kernel(node_hbm, owner_hbm, number_hbm, cache_hbm, pages_ref, node_row, owner_ref, number_ref, cache_ref, sems):
    copies = load((cache_hbm, node_hbm, owner_hbm, number_hbm), (cache_ref, node_row, owner_ref, number_ref), sems)
    for copy in copies[1:]:
        copy.wait()
    me = lax.axis_index("node")
    count = NODES * 8
    node_of = (iota((count, NODES), 0) // 8 + ROOT) % NODES
    within = iota((count, 1), 0) % 8
    slot = within // 2
    expand = (node_row[...] == node_of).astype(BF16)
    owner = mm(expand, owner_ref[...].reshape(NODES, MAXP).astype(BF16))
    number = mm(expand, number_ref[...].astype(BF16))
    held = owner == me.astype(F32)
    before = (iota((MAXP, MAXP), 0) < iota((MAXP, MAXP), 1)).astype(BF16)
    rank = mm(held.astype(BF16), before)
    picked = held & (rank == slot.astype(F32))
    page = jnp.sum(jnp.where(picked, number + 1.0, 0.0), axis=1, keepdims=True).astype(jnp.int32) - 1
    row = 2 * page + within % 2
    select = (iota((count, 128), 1) == row) & (page >= 0)
    copies[0].wait()
    pages_ref[:, :KEY] = mm(select.astype(BF16), cache_ref[...].reshape(128, KEY)).astype(BF16)
    pages_ref[:, KEY:] = jnp.zeros((count, PAGEW - KEY), BF16)


def add_kernel(keep_ref, *refs):
    *swapped_refs, out_ref = refs
    for (lo, hi), swapped_ref in zip(SENDS, swapped_refs):
        out_ref[:, lo:hi] = (keep_ref[:, lo:hi] + swapped_ref[...]).astype(BF16)


def angles(length, rows, cb_ref, sb_ref, ct_ref, st_ref):
    at = iota(cb_ref.shape, 0) == length
    cb = jnp.sum(jnp.where(at, cb_ref[...], 0.0), axis=0, keepdims=True)
    sb = jnp.sum(jnp.where(at, sb_ref[...], 0.0), axis=0, keepdims=True)
    ct = ct_ref[rows, :]
    st = st_ref[rows, :]
    return cb * ct - sb * st, sb * ct + cb * st


def turn(v):
    half = ROPE // 2
    parts = []
    for g in range(v.shape[1] // ROPE):
        parts.append(-v[:, g * ROPE + half : (g + 1) * ROPE])
        parts.append(v[:, g * ROPE : g * ROPE + half])
    return jnp.concatenate(parts, axis=1)


def finish_kernel(
    node_row,
    adapter_row,
    length_row,
    owner_ref,
    parts_ref,
    pages_ref,
    aq_ref,
    akv_ref,
    gq_ref,
    gkv_ref,
    cb_ref,
    sb_ref,
    ct_ref,
    st_ref,
    out_ref,
):
    me = lax.axis_index("node")
    adapter = mine_of(adapter_row, node_row)
    length = mine_of(length_row, node_row)
    core = lax.axis_index("tp") % 2
    chip = lax.axis_index("tp") // 2
    place = (chip // 4 + 4 - CORNER[0]) % 4 * 4 + (chip + 4 - CORNER[1]) % 4
    first = pl.multiple_of(core * HALF + place * ROWS, ROWS)
    down = parts_ref[0].astype(F32)
    for i in range(1, CHIPS):
        down = down + parts_ref[i].astype(F32)
    count = aq_ref.shape[0] * RANK
    chosen = iota((ROWS, count), 1) // RANK == adapter

    def raised(low, up_ref):
        low = jnp.where(chosen, jnp.concatenate([low] * aq_ref.shape[0], axis=1), 0.0).astype(BF16)
        return mm(low, up_ref[...].reshape(count, up_ref.shape[2]))

    q_raw = down[:, :Q] + raised(down[:, Q + KEY : Q + KEY + RANK], aq_ref)
    kv_raw = down[:, Q : Q + KEY] + raised(down[:, Q + KEY + RANK :], akv_ref)
    q_lat = q_raw * lax.rsqrt(jnp.mean(q_raw * q_raw, axis=1, keepdims=True) + 1e-06) * gq_ref[...][None, :]
    c = kv_raw[:, :LATENT]
    c = c * lax.rsqrt(jnp.mean(c * c, axis=1, keepdims=True) + 1e-06) * gkv_ref[...][None, :]
    k = kv_raw[:, LATENT:]
    cosine, sine = angles(length, pl.ds(first, ROWS), cb_ref, sb_ref, ct_ref, st_ref)
    k = k * cosine[:, :ROPE] + turn(k) * sine[:, :ROPE]

    count = MAXP * 2
    pick = (node_row[...] == me).astype(BF16)
    mine_owner = mm(pick, owner_ref[...].reshape(NODES, MAXP).astype(BF16))
    entry = iota((count, MAXP), 0) // 2
    lane = iota((count, MAXP), 1)
    holder = jnp.sum(jnp.where(lane == entry, mine_owner, 0.0), axis=1, keepdims=True)
    earlier = (mine_owner == holder) & (lane < entry)
    rank = jnp.sum(earlier.astype(F32), axis=1, keepdims=True)
    source = (holder.astype(jnp.int32) + (NODES - ROOT)) % NODES * 8 + rank.astype(jnp.int32) * 2 + iota((count, 1), 0) % 2
    select = (iota((count, 128), 1) == source).astype(BF16)
    prefix = mm(select, pages_ref[...])[:, :KEY]
    chunks = [prefix[g * ROWS : (g + 1) * ROWS] for g in range(CHUNKS)]
    pieces = [q_lat, c] + [p[:, :LATENT] for p in chunks]
    pieces += [k] + [p[:, LATENT:] for p in chunks] + [jnp.zeros((ROWS, ROPE), F32)]
    block = jnp.concatenate(pieces, axis=1).astype(BF16)
    for i in range(CHIPS):
        out_ref[i] = block


def attend_kernel(
    node_row, length_row, mine_ref, other_ref, wq_ref, wk_ref, wv_ref, cb_ref, sb_ref, ct_ref, st_ref, out_ref
):
    length = mine_of(length_row, node_row)
    core = lax.axis_index("tp") % 2
    rows_a = pl.ds(pl.multiple_of(core * HALF, HALF), HALF)
    rows_b = pl.ds(pl.multiple_of((1 - core) * HALF, HALF), HALF)

    def both(lo, hi):
        return jnp.concatenate([mine_ref[:, lo:hi], other_ref[:, lo:hi]], axis=0)

    q_all = mm(both(0, Q), wq_ref[...]).astype(BF16)
    ca, sa = angles(length, rows_a, cb_ref, sb_ref, ct_ref, st_ref)
    cb, sb = angles(length, rows_b, cb_ref, sb_ref, ct_ref, st_ref)
    cosine = jnp.concatenate([ca, cb], axis=0)
    sine = jnp.concatenate([sa, sb], axis=0)
    ropes = jnp.concatenate([q_all[:, NOPE:HEADW], q_all[:, HEADW + NOPE :]], axis=1).astype(F32)
    ropes = (ropes * cosine + turn(ropes) * sine).astype(BF16)
    rope = jnp.concatenate([ropes[:, :ROPE], ropes[:, ROPE:]], axis=0)
    zero = jnp.zeros_like(rope)
    absorbed = [mm(q_all[:, h * HEADW : h * HEADW + NOPE], wk_ref[h]).astype(BF16) for h in range(2)]
    absorbed = jnp.concatenate(absorbed, axis=0)
    query = (jnp.concatenate([absorbed, rope, zero], axis=1), jnp.concatenate([absorbed, zero, rope], axis=1))
    latents = [both(Q + g * LATENT, Q + (g + 1) * LATENT) for g in range(GROUPS)]

    count = 2 * SUFLEN
    place = iota((count, SUFLEN), 0) % SUFLEN
    place = jnp.where(place < HALF, place + core * HALF, place - core * HALF)
    spot = iota((count, SUFLEN), 1)
    page = (spot % 8) // 2
    spot = jnp.where(spot < HALF, spot + core * HALF, spot - core * HALF)
    scores = []
    for g in range(GROUPS):
        tile = ROPES + g // 2 * 128
        s = mmt(query[g % 2], jnp.concatenate([latents[g], both(tile, tile + 128)], axis=1))
        if g == 0:
            s = jnp.where(place >= spot, s, -jnp.inf)
        elif g > 2:
            s = jnp.where(page + 4 * (g - 1) < length, s, -jnp.inf)
        scores.append(s)
    top = scores[0]
    for s in scores[1:]:
        top = jnp.maximum(top, s)
    top = jnp.max(top, axis=1, keepdims=True)
    weights = [jnp.exp2((s - top) * FACTOR) for s in scores]
    total = weights[0]
    for w in weights[1:]:
        total = total + w
    total = jnp.sum(total, axis=1, keepdims=True)
    weights = jnp.concatenate([w.astype(BF16) for w in weights], axis=1)
    mixed = mm(weights, jnp.concatenate(latents, axis=0))
    latent = (mixed / total).astype(BF16)
    for h in range(2):
        values = mm(latent[h * SUFLEN : (h + 1) * SUFLEN], wv_ref[h]).astype(BF16)
        out_ref[rows_a, h * VDIM : (h + 1) * VDIM] = values[:HALF]
        out_ref[rows_b, h * VDIM : (h + 1) * VDIM] = values[HALF:]


def on_device(
    suffix_hidden,
    suffix_adapter,
    page_owner,
    page_number,
    prefix_page_count,
    suffix_node,
    prefix_cache,
    query_down_weight,
    kv_down_weight,
    adapter_down_panels,
    adapter_query_up,
    adapter_kv_up,
    latent_query_gain,
    latent_kv_gain,
    query_up_weight,
    key_up_weight,
    value_up_weight,
):
    params = pltpu.CompilerParams(vmem_limit_bytes=40 * 1024 * 1024)
    tables = [jnp.asarray(t) for t in rope_tables()]
    owner = jnp.transpose(page_owner, (0, 2, 1))
    node_row, adapter_row, length_row = [a.reshape(1, NODES) for a in (suffix_node, suffix_adapter, prefix_page_count)]

    def far(*arrays):
        return [pltpu.with_memory_space_constraint(a, pltpu.HBM) for a in arrays]

    swap = [(i, i ^ 1) for i in range(2 * CHIPS)]

    outgoing = pl.pallas_call(
        pages_kernel,
        out_shape=jax.ShapeDtypeStruct((NODES * 8, PAGEW), BF16),
        in_specs=[HBM] * 4,
        out_specs=VMEM,
        scratch_shapes=[
            pltpu.VMEM((1, NODES), jnp.int32),
            pltpu.VMEM((NODES, 1, MAXP), jnp.int32),
            pltpu.VMEM((NODES, MAXP), jnp.int32),
            pltpu.VMEM(prefix_cache.shape, BF16),
            pltpu.SemaphoreType.DMA((4,)),
        ],
        compiler_params=params,
        cost_estimate=pl.CostEstimate(flops=20_000_000, bytes_accessed=300_000, transcendentals=0),
        name="pages",
    )(*far(node_row, owner, page_number, prefix_cache))
    received = lax.all_to_all(outgoing.reshape(NODES, 8, PAGEW), "node", 0, 0, tiled=True, axis_index_groups=[RING])
    hidden, _ = lax.optimization_barrier((suffix_hidden, outgoing))
    keep, *send = pl.pallas_call(
        down_kernel,
        out_shape=[jax.ShapeDtypeStruct((HALF, DOWN), F32)] + [jax.ShapeDtypeStruct((HALF, hi - lo), F32) for lo, hi in SENDS],
        in_specs=[HBM] * 6,
        out_specs=[VMEM] * (1 + len(SENDS)),
        scratch_shapes=[
            pltpu.VMEM((1, NODES), jnp.int32),
            pltpu.VMEM((1, NODES), jnp.int32),
            pltpu.VMEM((224, SUFLEN), BF16),
            pltpu.VMEM((224, Q), BF16),
            pltpu.VMEM((224, KEY), BF16),
            pltpu.VMEM((4, 2 * RANK, 224), BF16),
            pltpu.SemaphoreType.DMA((6,)),
        ],
        compiler_params=params,
        cost_estimate=pl.CostEstimate(flops=1000, bytes_accessed=1000, transcendentals=0),
        name="down",
    )(*far(node_row, adapter_row, hidden.T, query_down_weight, kv_down_weight, jnp.transpose(adapter_down_panels, (0, 2, 1))))
    swapped = [lax.ppermute(part, "tp", swap) for part in send]
    partial = pl.pallas_call(
        add_kernel,
        out_shape=jax.ShapeDtypeStruct((HALF, DOWN), BF16),
        in_specs=[VMEM] * (1 + len(SENDS)),
        out_specs=VMEM,
        compiler_params=params,
        cost_estimate=pl.CostEstimate(flops=1000, bytes_accessed=1000, transcendentals=0),
        name="add",
    )(keep, *swapped).reshape(CHIPS, ROWS, DOWN)
    parts = lax.all_to_all(partial, "tp", 0, 0, tiled=True, axis_index_groups=PLANE)

    block = pl.pallas_call(
        finish_kernel,
        out_shape=jax.ShapeDtypeStruct((CHIPS, ROWS, BLOCK), BF16),
        in_specs=[VMEM] * 14,
        out_specs=VMEM,
        compiler_params=params,
        name="finish",
    )(
        node_row,
        adapter_row,
        length_row,
        owner,
        parts,
        received.reshape(NODES * 8, PAGEW),
        adapter_query_up,
        adapter_kv_up,
        latent_query_gain,
        latent_kv_gain,
        *tables,
    )
    gathered = lax.all_to_all(block, "tp", 0, 0, tiled=True, axis_index_groups=PLANE).reshape(HALF, BLOCK)
    other = lax.ppermute(gathered, "tp", swap)
    return pl.pallas_call(
        attend_kernel,
        out_shape=jax.ShapeDtypeStruct((SUFLEN, 2 * VDIM), BF16),
        in_specs=[VMEM] * 11,
        out_specs=VMEM,
        compiler_params=params,
        name="attend",
    )(
        node_row,
        length_row,
        gathered,
        other,
        query_up_weight,
        key_up_weight,
        value_up_weight,
        *tables,
    )


def solution(mesh):
    return jax.shard_map(
        on_device,
        mesh=mesh,
        in_specs=(
            P("node", "tp"),
            P(),
            P(),
            P(),
            P(),
            P(),
            P("node", "tp", None),
            P("tp", None),
            P("tp", None),
            P(None, "tp", None),
            P(),
            P(),
            P(),
            P(),
            P(None, "tp"),
            P("tp", None, None),
            P("tp", None, None),
        ),
        out_specs=P("node", "tp"),
        check_vma=False,
    )
```
